32 devices in a mesh: dom: 32 (over z, y, x, core).
Axes of the slice: x: 2, y: 2, z: 4, core: 2. Of those that a mesh axis runs over, the one named last changes fastest.
Arguments:
- embeddings: float32 [16384, 400], P('dom'), may hold values from -1.8 to 1.8
- row_state: float32 [16384], P('dom'), may hold values from 0.01 to 1
- relations: float32 [2048, 400], P('dom'), may hold values from 0.5 to 1.5
- relation_state: float32 [2048], P('dom'), may hold values from 0.01 to 1
- partner_mask: int32 [1], replicated, may hold values from 1 to 31
- source_rows: int32 [98304], P('dom'), may hold values from 0 to 511
- relation_ids: int32 [98304], P('dom'), may hold values from 0 to 2047
- dest_rows: int32 [98304], P('dom'), may hold values from 0 to 511
- negative_rows: int32 [384, 512], P('dom'), may hold values from 0 to 511
- edge_count: int32 [32], P('dom'), may hold values from 1 to 3072, 61440 in all
Outputs:
- new_embeddings: float32 [16384, 400], P('dom')
- new_row_state: float32 [16384], P('dom')
- new_relations: float32 [2048, 400], P('dom')
- new_relation_state: float32 [2048], P('dom')
The draws below stay inside these ranges and needn't reach their ends.
Inputs may be any that keep to these rules, and one draw needn't show every extreme that they name: Device i trains the bucket of partition i with partition i XOR partner_mask[0]. `edge_count`: some bucket has all 3072 slots live.
All inputs are finite; a program needn't handle non-finite values. No bound on the sum of `edge_count` on one device may be relied on, other than what follows from the above.
Results may differ from the reference program's by a relative error of at most 0.0015.
Values may be sent and summed in bfloat16 or wider, within the bound.
A program may use at most 128 MiB of HBM per device.

```python
import math
import jax
import jax.numpy as jnp
import numpy as np
from jax import lax

D = 400
RELS = 2048
ROWS = 512
EDGES = 3072
NEGS = 512
GROUPS = 12
ALL_ROWS = 16384
ALL_EDGES = 98304
ALL_GROUPS = 384
N_DOM = 32


def touch_ends(array, rng, low, largest):
    shape = array.shape
    index_at = [jax.random.randint(jax.random.fold_in(rng, axis), (), 0, shape[axis]) for axis in range(len(shape))]
    array = array.at[tuple(index_at)].set(low)
    longest = shape.index(max(shape))
    index_at[longest] = (index_at[longest] + 1) % shape[longest]
    return array.at[tuple(index_at)].set(largest)


def block_scale(key, dims, shards, smallest, largest):
    level = 1.0
    for axis_at, blocks in shards:
        steps = jax.random.uniform(jax.random.fold_in(jax.random.fold_in(key, 6), axis_at), (blocks,), jnp.float32, smallest / len(shards), largest / len(shards))
        level = level * jnp.repeat(jnp.exp(steps), dims[axis_at] // blocks).reshape((-1,) + (1,) * (len(dims) - 1 - axis_at))
    return level


def rank_table(amount, skew):
    loads = [(1 << 20) // math.isqrt(grade ** skew) + 1 for grade in range(1, amount + 1)]
    scale = 1 + sum(loads) // (1 << 30)
    return np.cumsum(np.array([max(1, weight // scale) for weight in loads]))


def ranked(stream_key, extent, number_of, slope):
    listing = rank_table(number_of, slope)
    ticket = jax.random.randint(jax.random.fold_in(stream_key, 1), extent, 0, int(listing[number_of - 1]))
    rank = jnp.searchsorted(jnp.asarray(listing, jnp.int32), ticket, side="right")
    return jax.random.permutation(jax.random.fold_in(stream_key, 2), number_of)[rank].astype(jnp.int32)


def length_profile(number_of, total, reach, skew):
    loads = [(1 << 20) // math.isqrt(rank ** skew) + 1 for rank in range(2, number_of + 1)]
    rest, given = total - reach - (number_of - 1), [1] * (number_of - 1)
    while rest > 0:
        free = [i for i in range(number_of - 1) if given[i] < reach]
        pool, budget = sum([loads[i] for i in free]), rest
        for i in free:
            addition = min(reach - given[i], max(1, budget * loads[i] // pool), rest)
            given[i] = given[i] + addition
            rest = rest - addition
    return np.array([reach] + given)


def ragged(stream_key, count, total, bound, lean):
    if count == 2:
        one = jax.random.randint(stream_key, (), max(1, total - bound), min(bound, total - 1) + 1)
        return jnp.stack([one, total - one])
    lengths = jnp.asarray(length_profile(count, total, bound, lean), jnp.int32)
    twos = (count - 1) // 2
    giver, receiver = lengths[1:1 + 2 * twos:2], lengths[2:2 + 2 * twos:2]
    slack = jnp.minimum(giver - 1, bound - receiver)
    moved = jax.random.randint(jax.random.fold_in(stream_key, 1), (twos,), 0, 1 << 20) % (slack + 1)
    lengths = lengths.at[1:1 + 2 * twos:2].set(giver - moved).at[2:2 + 2 * twos:2].set(receiver + moved)
    return lengths[jax.random.permutation(jax.random.fold_in(stream_key, 2), count)]


def gaussian(key, dims, deviation, limit, pieces=(), kind=jnp.bfloat16):
    factor_of = block_scale(key, dims, pieces, -0.22, 0.18) if pieces else 1.0
    result = jax.random.normal(key, dims, jnp.float32) * deviation * factor_of
    return jnp.minimum(jnp.maximum(result, -limit), limit).astype(kind)


def setup_inputs(seed: int = 0) -> dict:
    key_list = jax.random.split(jax.random.key(seed), 11)
    return {
        "embeddings": gaussian(key_list[0], (ALL_ROWS, D), 0.3, 1.8, ((0, 32),), jnp.float32),
        "row_state": jnp.clip(jnp.exp(math.log(1.0) - 4.6051702 * jax.random.uniform(key_list[1], (ALL_ROWS,), jnp.float32) ** block_scale(key_list[1], (ALL_ROWS,), ((0, 32),), -0.2, 0.2)), 0.01, 1.0),
        "relations": jnp.clip(1.0 + 0.1 * jax.random.normal(key_list[2], (RELS, D), jnp.float32), 0.5, 1.5),
        "relation_state": jnp.clip(jnp.exp(math.log(1.0) - 4.6051702 * jax.random.uniform(key_list[3], (RELS,), jnp.float32) ** block_scale(key_list[3], (RELS,), ((0, 32),), -0.2, 0.2)), 0.01, 1.0),
        "partner_mask": jax.random.randint(key_list[4], (1,), 1, N_DOM).astype(jnp.int32),
        "source_rows": touch_ends(jax.random.randint(key_list[5], (ALL_EDGES,), 0, ROWS), jax.random.fold_in(key_list[5], 1), 0, ROWS - 1).astype(jnp.int32),
        "relation_ids": touch_ends(ranked(key_list[6], (ALL_EDGES,), RELS, 1), jax.random.fold_in(key_list[6], 3), 0, RELS - 1).astype(jnp.int32),
        "dest_rows": touch_ends(jax.random.randint(key_list[7], (ALL_EDGES,), 0, ROWS), jax.random.fold_in(key_list[7], 1), 0, ROWS - 1).astype(jnp.int32),
        "negative_rows": touch_ends(jax.random.randint(key_list[8], (ALL_GROUPS, NEGS), 0, ROWS), jax.random.fold_in(key_list[8], 1), 0, ROWS - 1).astype(jnp.int32),
        "edge_count": ragged(key_list[9], N_DOM, EDGES * N_DOM * 5 // 8, EDGES, 2).astype(jnp.int32),
    }


def train_bucket(own_bf, part_bf, rel_bf, source, rel_ids, target_rows, negatives, live_count):
    groups, negs_per = negatives.shape
    edges = source.shape[0]
    group_len = edges // groups
    width = own_bf.shape[1]
    own_rows = own_bf[source].astype(jnp.float32)
    rel_rows = rel_bf[rel_ids].astype(jnp.float32)
    queries = (own_rows * rel_rows).astype(jnp.bfloat16)
    query_full = queries.astype(jnp.float32)
    targets = part_bf[target_rows].astype(jnp.float32)
    positive = lax.optimization_barrier(jnp.sum(query_full * targets, axis=1))
    sampled = part_bf[negatives].astype(jnp.float32)
    grouped = query_full.reshape(groups, group_len, width)
    scores = jnp.einsum('gkd,gnd->gkn', grouped, sampled)
    live = (jnp.arange(edges, dtype=jnp.int32) < live_count).astype(jnp.float32)
    pos_grad = -live * jax.nn.sigmoid(-positive)
    neg_grad = (live.reshape(groups, group_len, 1) * jax.nn.sigmoid(scores) / negs_per).astype(jnp.bfloat16)
    neg_full = neg_grad.astype(jnp.float32)
    query_grad = pos_grad[:, None] * targets + jnp.einsum('gkn,gnd->gkd', neg_full, sampled).reshape(edges, width)
    own_grad = jnp.zeros((own_bf.shape[0], width), jnp.float32).at[source].add(query_grad * rel_rows)
    rel_grad = jnp.zeros((rel_bf.shape[0], width), jnp.float32).at[rel_ids].add(query_grad * own_rows)
    neg_terms = jnp.einsum('gkn,gkd->gnd', neg_full, grouped).reshape(groups * negs_per, width)
    part_grad = jnp.zeros((part_bf.shape[0], width), jnp.float32).at[target_rows].add(pos_grad[:, None] * query_full)
    part_grad = part_grad.at[negatives.reshape(-1)].add(neg_terms)
    return (own_grad, part_grad.astype(jnp.bfloat16), rel_grad)

def reference(embeddings, row_state, relations, relation_state, partner_mask, source_rows, relation_ids, dest_rows, negative_rows, edge_count):
    blocks = embeddings.astype(jnp.bfloat16).reshape(N_DOM, ROWS, D)
    rel_bf = relations.astype(jnp.bfloat16)
    partner = jnp.bitwise_xor(jnp.arange(N_DOM, dtype=jnp.int32), partner_mask[0])
    sources = source_rows.reshape(N_DOM, EDGES)
    rel_all = relation_ids.reshape(N_DOM, EDGES)
    targets = dest_rows.reshape(N_DOM, EDGES)
    negatives = negative_rows.reshape(N_DOM, GROUPS, NEGS)

    def visit(summed, device):
        own_grad, part_grad, rel_grad = train_bucket(blocks[device], blocks[partner[device]], rel_bf, sources[device], rel_all[device], targets[device], negatives[device], edge_count[device])
        return (summed + rel_grad, (own_grad, part_grad))
    rel_total, (own_grads, part_grads) = lax.scan(visit, jnp.zeros((RELS, D), jnp.float32), jnp.arange(N_DOM, dtype=jnp.int32))
    grad = (own_grads + part_grads[partner].astype(jnp.float32)).reshape(ALL_ROWS, D)
    new_row_state = row_state + lax.optimization_barrier(jnp.mean(grad * grad, axis=1))
    new_embeddings = embeddings - 0.1 * grad / jnp.sqrt(new_row_state)[:, None]
    new_relation_state = relation_state + lax.optimization_barrier(jnp.mean(rel_total * rel_total, axis=1))
    new_relations = relations - 0.1 * rel_total / jnp.sqrt(new_relation_state)[:, None]
    return (new_embeddings, new_row_state, new_relations, new_relation_state)
```

```python
import functools

import jax
import jax.numpy as jnp
from jax import lax
from jax.experimental import pallas as pl
from jax.experimental.pallas import tpu as pltpu
from jax.sharding import PartitionSpec as P

BF = jnp.bfloat16
F32 = jnp.float32


def nn(a, b):
    return lax.dot_general(a, b, (((1,), (0,)), ((), ())), preferred_element_type=F32)


def nt(a, b):
    return lax.dot_general(a, b, (((1,), (1,)), ((), ())), preferred_element_type=F32)


def one_hot(rows, ids, first=0):
    at = lax.broadcasted_iota(jnp.int32, (rows, ids.shape[1]), 0) + first
    return at == ids


def as_bf(mask):
    return jnp.where(mask, 1.0, 0.0).astype(BF)


def sigmoid(x):
    return 0.5 * jnp.tanh(0.5 * x) + 0.5


def bucket_kernel(
    count_ref,
    own_ref,
    part_ref,
    rel_ref,
    source_ref,
    ids_ref,
    dest_ref,
    negs_ref,
    own_grad_ref,
    part_grad_ref,
    rel_grad_ref,
    own_t,
    part_t,
    rel_t,
    y_t,
    part_acc,
):
    groups, _, group_len = source_ref.shape
    negs_per = negs_ref.shape[2]
    rows, width = own_ref.shape
    rels = rel_ref.shape[0]
    eye = as_bf(
        lax.broadcasted_iota(jnp.int32, (width, width), 0)
        == lax.broadcasted_iota(jnp.int32, (width, width), 1)
    )
    own_t[...] = nt(eye, own_ref[...].astype(BF)).astype(BF)
    part_t[...] = nt(eye, part_ref[...]).astype(BF)
    rel_t[...] = nt(eye, rel_ref[...]).astype(BF)
    own_grad_ref[...] = jnp.zeros_like(own_grad_ref)
    part_acc[...] = jnp.zeros_like(part_acc)
    count = count_ref[0]

    def group(g, carry):
        from_source = as_bf(one_hot(rows, source_ref[g]))
        own_rows = nn(own_t[...], from_source)
        rel_rows = nn(rel_t[...], as_bf(one_hot(rels, ids_ref[g])))
        queries = (own_rows * rel_rows).astype(BF)
        scores = nn(part_ref[...], queries)
        to_dest = one_hot(rows, dest_ref[g])
        positive = jnp.sum(jnp.where(to_dest, scores, 0.0), axis=0, keepdims=True)
        edge = lax.broadcasted_iota(jnp.int32, (1, group_len), 1) + g * group_len
        live = jnp.where(edge < count, 1.0, 0.0)
        pos_grad = -live * sigmoid(-positive)
        times = jnp.sum(
            jnp.where(one_hot(rows, negs_ref[g]), 1.0 / negs_per, 0.0), axis=1, keepdims=True
        )
        weight = times * (live * sigmoid(scores)) + jnp.where(to_dest, pos_grad, 0.0)
        high = weight.astype(BF)
        low = jnp.where(to_dest, weight - high.astype(F32), 0.0).astype(BF)
        query_grad = nn(part_t[...], high) + nn(part_t[...], low)
        part_acc[...] += nt(high, queries) + nt(low, queries)
        own_grad_ref[...] += nt(from_source, (query_grad * rel_rows).astype(BF))
        columns = pl.ds(pl.multiple_of(g * group_len, group_len), group_len)
        y_t[:, columns] = (query_grad * own_rows).astype(BF)
        return carry

    lax.fori_loop(0, groups, group, 0)
    part_grad_ref[...] = part_acc[...].astype(BF)

    chunk = min(rels, rows)

    def scatter(c, carry):
        first = pl.multiple_of(c * chunk, chunk)
        total = jnp.zeros((chunk, width), F32)
        for g in range(groups):
            hot = as_bf(one_hot(chunk, ids_ref[g], first))
            total = total + nt(hot, y_t[:, g * group_len : (g + 1) * group_len])
        rel_grad_ref[pl.ds(first, chunk), :] = total
        return carry

    lax.fori_loop(0, rels // chunk, scatter, 0)


def train_bucket(embeddings, part_bf, rel_bf, source, rel_ids, dest, negatives, count):
    groups, negs_per = negatives.shape
    edges = source.shape[0]
    rows, width = embeddings.shape
    rels = rel_bf.shape[0]
    split = (groups, 1, edges // groups)
    vmem = pl.BlockSpec(memory_space=pltpu.VMEM)
    unit = 2 * edges * rows * width
    return pl.pallas_call(
        bucket_kernel,
        out_shape=(
            jax.ShapeDtypeStruct((rows, width), F32),
            jax.ShapeDtypeStruct((rows, width), BF),
            jax.ShapeDtypeStruct((rels, width), F32),
        ),
        in_specs=[pl.BlockSpec(memory_space=pltpu.SMEM)] + [vmem] * 7,
        out_specs=(vmem,) * 3,
        scratch_shapes=[
            pltpu.VMEM((width, rows), BF),
            pltpu.VMEM((width, rows), BF),
            pltpu.VMEM((width, rels), BF),
            pltpu.VMEM((width, edges), BF),
            pltpu.VMEM((rows, width), F32),
        ],
        compiler_params=pltpu.CompilerParams(vmem_limit_bytes=50 * 2**20),
        cost_estimate=pl.CostEstimate(
            flops=7 * unit + 2 * unit * rels // rows,
            bytes_accessed=8 * (rows + rels) * width,
            transcendentals=edges * rows,
        ),
        name="bucket",
    )(
        count,
        embeddings,
        part_bf,
        rel_bf,
        source.reshape(split),
        rel_ids.reshape(split),
        dest.reshape(split),
        negatives.reshape(groups, 1, negs_per),
    )


def exchange(value, mask, axis):
    size = lax.axis_size(axis)

    def with_mask(m):
        pairs = [(i, i ^ m) for i in range(size)]
        return lambda v: lax.ppermute(v, axis, pairs)

    return lax.switch(mask - 1, [with_mask(m) for m in range(1, size)], value)


def adagrad(value, state, grad):
    new_state = state + jnp.mean(grad * grad, axis=1)
    return value - 0.1 * grad / jnp.sqrt(new_state)[:, None], new_state


def local(
    embeddings,
    row_state,
    relations,
    relation_state,
    partner_mask,
    source_rows,
    relation_ids,
    dest_rows,
    negative_rows,
    edge_count,
):
    mask = partner_mask[0]
    rel_bf = lax.all_gather(relations.astype(BF), "dom", axis=0, tiled=True)
    part_bf = exchange(embeddings.astype(BF), mask, "dom")
    own_grad, part_grad, rel_grad = train_bucket(
        embeddings, part_bf, rel_bf, source_rows, relation_ids, dest_rows, negative_rows, edge_count
    )
    rel_share = lax.psum_scatter(rel_grad, "dom", scatter_dimension=0, tiled=True)
    returned = exchange(part_grad, mask, "dom")
    new_embeddings, new_row_state = adagrad(
        embeddings, row_state, own_grad + returned.astype(F32)
    )
    new_relations, new_relation_state = adagrad(relations, relation_state, rel_share)
    return (new_embeddings, new_row_state, new_relations, new_relation_state)


def solution(mesh):
    in_specs = (
        P("dom", None),
        P("dom"),
        P("dom", None),
        P("dom"),
        P(),
        P("dom"),
        P("dom"),
        P("dom"),
        P("dom", None),
        P("dom"),
    )
    out_specs = (P("dom", None), P("dom"), P("dom", None), P("dom"))
    return jax.shard_map(local, mesh=mesh, in_specs=in_specs, out_specs=out_specs, check_vma=False)
```

```python
import functools

import jax
import jax.numpy as jnp
from jax import lax
from jax.experimental import pallas as pl
from jax.experimental.pallas import tpu as pltpu
from jax.sharding import PartitionSpec as P

BF = jnp.bfloat16
F32 = jnp.float32


def nn(a, b):
    return lax.dot_general(a, b, (((1,), (0,)), ((), ())), preferred_element_type=F32)


def nt(a, b):
    return lax.dot_general(a, b, (((1,), (1,)), ((), ())), preferred_element_type=F32)


def one_hot(rows, ids, first=0):
    at = lax.broadcasted_iota(jnp.int32, (rows, ids.shape[1]), 0) + first
    return at == ids


def as_bf(mask):
    return jnp.where(mask, 1.0, 0.0).astype(BF)


def sigmoid(x):
    return 0.5 * jnp.tanh(0.5 * x) + 0.5


def bucket_kernel(
    count_ref,
    own_ref,
    part_ref,
    rel_ref,
    source_ref,
    ids_ref,
    dest_ref,
    negs_ref,
    own_grad_ref,
    part_grad_ref,
    rel_grad_ref,
    own_t,
    part_t,
    rel_t,
    y_t,
    part_acc,
):
    groups, _, group_len = source_ref.shape
    negs_per = negs_ref.shape[2]
    rows, width = own_ref.shape
    rels = rel_ref.shape[0]
    eye = as_bf(
        lax.broadcasted_iota(jnp.int32, (width, width), 0)
        == lax.broadcasted_iota(jnp.int32, (width, width), 1)
    )
    own_t[...] = nt(eye, own_ref[...].astype(BF)).astype(BF)
    part_t[...] = nt(eye, part_ref[...]).astype(BF)
    rel_t[...] = nt(eye, rel_ref[...]).astype(BF)
    own_grad_ref[...] = jnp.zeros_like(own_grad_ref)
    part_acc[...] = jnp.zeros_like(part_acc)
    count = count_ref[0]

    def group(g, carry):
        from_source = as_bf(one_hot(rows, source_ref[g]))
        own_rows = nn(own_t[...], from_source)
        rel_rows = nn(rel_t[...], as_bf(one_hot(rels, ids_ref[g])))
        queries = (own_rows * rel_rows).astype(BF)
        scores = nn(part_ref[...], queries)
        to_dest = one_hot(rows, dest_ref[g])
        positive = jnp.sum(jnp.where(to_dest, scores, 0.0), axis=0, keepdims=True)
        edge = lax.broadcasted_iota(jnp.int32, (1, group_len), 1) + g * group_len
        live = jnp.where(edge < count, 1.0, 0.0)
        pos_grad = -live * sigmoid(-positive)
        times = jnp.sum(
            jnp.where(one_hot(rows, negs_ref[g]), 1.0 / negs_per, 0.0), axis=1, keepdims=True
        )
        weight = times * (live * sigmoid(scores)) + jnp.where(to_dest, pos_grad, 0.0)
        high = weight.astype(BF)
        low = jnp.where(to_dest, weight - high.astype(F32), 0.0).astype(BF)
        query_grad = nn(part_t[...], high) + nn(part_t[...], low)
        part_acc[...] += nt(high, queries) + nt(low, queries)
        own_grad_ref[...] += nt(from_source, (query_grad * rel_rows).astype(BF))
        columns = pl.ds(pl.multiple_of(g * group_len, group_len), group_len)
        y_t[:, columns] = (query_grad * own_rows).astype(BF)
        return carry

    lax.fori_loop(0, groups, group, 0)
    part_grad_ref[...] = part_acc[...].astype(BF)

    chunk = min(rels, rows)

    def scatter(c, carry):
        first = pl.multiple_of(c * chunk, chunk)
        total = jnp.zeros((chunk, width), F32)
        for g in range(groups):
            hot = as_bf(one_hot(chunk, ids_ref[g], first))
            total = total + nt(hot, y_t[:, g * group_len : (g + 1) * group_len])
        rel_grad_ref[pl.ds(first, chunk), :] = total
        return carry

    lax.fori_loop(0, rels // chunk, scatter, 0)


def train_bucket(embeddings, part_bf, rel_bf, source, rel_ids, dest, negatives, count):
    groups, negs_per = negatives.shape
    edges = source.shape[0]
    rows, width = embeddings.shape
    rels = rel_bf.shape[0]
    split = (groups, 1, edges // groups)
    vmem = pl.BlockSpec(memory_space=pltpu.VMEM)
    unit = 2 * edges * rows * width
    return pl.pallas_call(
        bucket_kernel,
        out_shape=(
            jax.ShapeDtypeStruct((rows, width), F32),
            jax.ShapeDtypeStruct((rows, width), BF),
            jax.ShapeDtypeStruct((rels, width), F32),
        ),
        in_specs=[pl.BlockSpec(memory_space=pltpu.SMEM)] + [vmem] * 7,
        out_specs=(vmem,) * 3,
        scratch_shapes=[
            pltpu.VMEM((width, rows), BF),
            pltpu.VMEM((width, rows), BF),
            pltpu.VMEM((width, rels), BF),
            pltpu.VMEM((width, edges), BF),
            pltpu.VMEM((rows, width), F32),
        ],
        compiler_params=pltpu.CompilerParams(vmem_limit_bytes=50 * 2**20),
        cost_estimate=pl.CostEstimate(
            flops=7 * unit + 2 * unit * rels // rows,
            bytes_accessed=8 * (rows + rels) * width,
            transcendentals=edges * rows,
        ),
        name="bucket",
    )(
        count,
        embeddings,
        part_bf,
        rel_bf,
        source.reshape(split),
        rel_ids.reshape(split),
        dest.reshape(split),
        negatives.reshape(groups, 1, negs_per),
    )


def flip(me, bit):
    return me + bit * (1 - 2 * ((me // bit) % 2))


def bit_order(me, bits):
    order = [2**t for t in range(bits)]
    if bits > 2:
        core = me % 2
        order[1], order[2] = 2 + 2 * core, 4 - 2 * core
    return order


def slot_of(device, bits):
    slot = device * 0
    for bit in bit_order(device, bits):
        slot = 2 * slot + (device // bit) % 2
    return slot


def greet(me, bits):
    barrier = pltpu.get_barrier_semaphore()
    for t in range(bits):
        pl.semaphore_signal(
            barrier, inc=1, device_id=(flip(me, 2**t),), device_id_type=pl.DeviceIdType.MESH
        )
    pl.semaphore_wait(barrier, bits)


def gather_kernel(bits, shard_ref, out_ref, send_sem, recv_sem):
    me = lax.axis_index("dom")
    slot = slot_of(me, bits)
    order = bit_order(me, bits)
    out_ref[slot] = shard_ref[...]
    greet(me, bits)
    for step in range(bits):
        held = 2**step
        blocks = out_ref.at[pl.ds((slot // held) * held, held)]
        copy = pltpu.make_async_remote_copy(
            src_ref=blocks,
            dst_ref=blocks,
            send_sem=send_sem.at[step],
            recv_sem=recv_sem.at[step],
            device_id=(flip(me, order[bits - 1 - step]),),
            device_id_type=pl.DeviceIdType.MESH,
        )
        copy.start()
        copy.wait()


def gather_relations(shard, size):
    bits = size.bit_length() - 1
    vmem = pl.BlockSpec(memory_space=pltpu.VMEM)
    return pl.pallas_call(
        functools.partial(gather_kernel, bits),
        out_shape=jax.ShapeDtypeStruct((size,) + shard.shape, shard.dtype),
        in_specs=[vmem],
        out_specs=vmem,
        scratch_shapes=[pltpu.SemaphoreType.DMA((bits,)), pltpu.SemaphoreType.DMA((bits,))],
        compiler_params=pltpu.CompilerParams(
            collective_id=0, has_side_effects=True, vmem_limit_bytes=32 * 2**20
        ),
        name="gather_relations",
    )(shard)


def sum_kernel(bits, grad_ref, out_ref, acc, outgoing, incoming, send_sem, recv_sem):
    me = lax.axis_index("dom")
    order = bit_order(me, bits)
    greet(me, bits)
    source, first = grad_ref, 0
    for step in range(bits):
        half = 2 ** (bits - 1 - step)
        at = 2**bits - 2 * half
        mine = (me // order[step]) % 2
        region = pl.ds(at, half)
        outgoing[region] = source[pl.ds(first + (1 - mine) * half, half)].astype(BF)
        copy = pltpu.make_async_remote_copy(
            src_ref=outgoing.at[region],
            dst_ref=incoming.at[region],
            send_sem=send_sem.at[step],
            recv_sem=recv_sem.at[step],
            device_id=(flip(me, order[step]),),
            device_id_type=pl.DeviceIdType.MESH,
        )
        copy.start()
        copy.wait()
        acc[region] = source[pl.ds(first + mine * half, half)] + incoming[region].astype(F32)
        source, first = acc, at
    out_ref[...] = acc[2**bits - 2]


def sum_relations(grad, size):
    bits = size.bit_length() - 1
    shard = grad.shape[1:]
    vmem = pl.BlockSpec(memory_space=pltpu.VMEM)
    return pl.pallas_call(
        functools.partial(sum_kernel, bits),
        out_shape=jax.ShapeDtypeStruct(shard, F32),
        in_specs=[vmem],
        out_specs=vmem,
        scratch_shapes=[
            pltpu.VMEM(grad.shape, F32),
            pltpu.VMEM(grad.shape, BF),
            pltpu.VMEM(grad.shape, BF),
            pltpu.SemaphoreType.DMA((bits,)),
            pltpu.SemaphoreType.DMA((bits,)),
        ],
        compiler_params=pltpu.CompilerParams(
            collective_id=1, has_side_effects=True, vmem_limit_bytes=50 * 2**20
        ),
        name="sum_relations",
    )(grad)


def exchange(value, mask, axis):
    size = lax.axis_size(axis)

    def with_mask(m):
        pairs = [(i, i ^ m) for i in range(size)]
        return lambda v: lax.ppermute(v, axis, pairs)

    return lax.switch(mask - 1, [with_mask(m) for m in range(1, size)], value)


def adagrad(value, state, grad):
    new_state = state + jnp.mean(grad * grad, axis=1)
    return value - 0.1 * grad / jnp.sqrt(new_state)[:, None], new_state


def local(
    embeddings,
    row_state,
    relations,
    relation_state,
    partner_mask,
    source_rows,
    relation_ids,
    dest_rows,
    negative_rows,
    edge_count,
):
    mask = partner_mask[0]
    size = lax.axis_size("dom")
    share, width = relations.shape
    rel_bf = gather_relations(relations.astype(BF), size).reshape(size * share, width)
    slots = slot_of(relation_ids // share, size.bit_length() - 1) * share + relation_ids % share
    part_bf = exchange(embeddings.astype(BF), mask, "dom")
    own_grad, part_grad, rel_grad = train_bucket(
        embeddings, part_bf, rel_bf, source_rows, slots, dest_rows, negative_rows, edge_count
    )
    rel_share = sum_relations(rel_grad.reshape(size, share, width), size)
    returned = exchange(part_grad, mask, "dom")
    new_embeddings, new_row_state = adagrad(
        embeddings, row_state, own_grad + returned.astype(F32)
    )
    new_relations, new_relation_state = adagrad(relations, relation_state, rel_share)
    return (new_embeddings, new_row_state, new_relations, new_relation_state)


def solution(mesh):
    in_specs = (
        P("dom", None),
        P("dom"),
        P("dom", None),
        P("dom"),
        P(),
        P("dom"),
        P("dom"),
        P("dom"),
        P("dom", None),
        P("dom"),
    )
    out_specs = (P("dom", None), P("dom"), P("dom", None), P("dom"))
    return jax.shard_map(local, mesh=mesh, in_specs=in_specs, out_specs=out_specs, check_vma=False)
```

```python
import functools

import jax
import jax.numpy as jnp
from jax import lax
from jax.experimental import pallas as pl
from jax.experimental.pallas import tpu as pltpu
from jax.sharding import PartitionSpec as P

BF = jnp.bfloat16
F32 = jnp.float32


def nn(a, b):
    return lax.dot_general(a, b, (((1,), (0,)), ((), ())), preferred_element_type=F32)


def nt(a, b):
    return lax.dot_general(a, b, (((1,), (1,)), ((), ())), preferred_element_type=F32)


def one_hot(rows, ids, first=0):
    at = lax.broadcasted_iota(jnp.int32, (rows, ids.shape[1]), 0) + first
    return at == ids


def as_bf(mask):
    return jnp.where(mask, 1.0, 0.0).astype(BF)


def sigmoid(x):
    return 0.5 * jnp.tanh(0.5 * x) + 0.5


def bucket_kernel(
    count_ref,
    own_ref,
    part_ref,
    rel_ref,
    source_ref,
    ids_ref,
    dest_ref,
    negs_ref,
    own_grad_ref,
    part_grad_ref,
    rel_grad_ref,
    own_t,
    part_t,
    rel_t,
    y_t,
    part_acc,
):
    groups, _, group_len = source_ref.shape
    negs_per = negs_ref.shape[2]
    rows, width = own_ref.shape
    rels = rel_ref.shape[0]
    eye = as_bf(
        lax.broadcasted_iota(jnp.int32, (width, width), 0)
        == lax.broadcasted_iota(jnp.int32, (width, width), 1)
    )
    own_t[...] = nt(eye, own_ref[...].astype(BF)).astype(BF)
    part_t[...] = nt(eye, part_ref[...]).astype(BF)
    rel_t[...] = nt(eye, rel_ref[...]).astype(BF)
    own_grad_ref[...] = jnp.zeros_like(own_grad_ref)
    part_acc[...] = jnp.zeros_like(part_acc)
    count = count_ref[0]

    def group(g, carry):
        from_source = as_bf(one_hot(rows, source_ref[g]))
        own_rows = nn(own_t[...], from_source)
        rel_rows = nn(rel_t[...], as_bf(one_hot(rels, ids_ref[g])))
        queries = (own_rows * rel_rows).astype(BF)
        scores = nn(part_ref[...], queries)
        to_dest = one_hot(rows, dest_ref[g])
        positive = jnp.sum(jnp.where(to_dest, scores, 0.0), axis=0, keepdims=True)
        edge = lax.broadcasted_iota(jnp.int32, (1, group_len), 1) + g * group_len
        live = jnp.where(edge < count, 1.0, 0.0)
        pos_grad = -live * sigmoid(-positive)
        times = jnp.sum(
            jnp.where(one_hot(rows, negs_ref[g]), 1.0 / negs_per, 0.0), axis=1, keepdims=True
        )
        weight = times * (live * sigmoid(scores)) + jnp.where(to_dest, pos_grad, 0.0)
        high = weight.astype(BF)
        low = jnp.where(to_dest, weight - high.astype(F32), 0.0).astype(BF)
        query_grad = nn(part_t[...], high) + nn(part_t[...], low)
        part_acc[...] += nt(high, queries) + nt(low, queries)
        own_grad_ref[...] += nt(from_source, (query_grad * rel_rows).astype(BF))
        columns = pl.ds(pl.multiple_of(g * group_len, group_len), group_len)
        y_t[:, columns] = (query_grad * own_rows).astype(BF)
        return carry

    lax.fori_loop(0, groups, group, 0)
    part_grad_ref[...] = part_acc[...].astype(BF)

    chunk = min(rels, rows)

    def scatter(c, carry):
        first = pl.multiple_of(c * chunk, chunk)
        total = jnp.zeros((chunk, width), F32)
        for g in range(groups):
            hot = as_bf(one_hot(chunk, ids_ref[g], first))
            total = total + nt(hot, y_t[:, g * group_len : (g + 1) * group_len])
        rel_grad_ref[pl.ds(first, chunk), :] = total
        return carry

    lax.fori_loop(0, rels // chunk, scatter, 0)


def train_bucket(embeddings, part_bf, rel_bf, source, rel_ids, dest, negatives, count):
    groups, negs_per = negatives.shape
    edges = source.shape[0]
    rows, width = embeddings.shape
    rels = rel_bf.shape[0]
    split = (groups, 1, edges // groups)
    vmem = pl.BlockSpec(memory_space=pltpu.VMEM)
    unit = 2 * edges * rows * width
    return pl.pallas_call(
        bucket_kernel,
        out_shape=(
            jax.ShapeDtypeStruct((rows, width), F32),
            jax.ShapeDtypeStruct((rows, width), BF),
            jax.ShapeDtypeStruct((rels, width), F32),
        ),
        in_specs=[pl.BlockSpec(memory_space=pltpu.SMEM)] + [vmem] * 7,
        out_specs=(vmem,) * 3,
        scratch_shapes=[
            pltpu.VMEM((width, rows), BF),
            pltpu.VMEM((width, rows), BF),
            pltpu.VMEM((width, rels), BF),
            pltpu.VMEM((width, edges), BF),
            pltpu.VMEM((rows, width), F32),
        ],
        compiler_params=pltpu.CompilerParams(vmem_limit_bytes=50 * 2**20),
        cost_estimate=pl.CostEstimate(
            flops=7 * unit + 2 * unit * rels // rows,
            bytes_accessed=8 * (rows + rels) * width,
            transcendentals=edges * rows,
        ),
        name="bucket",
    )(
        count,
        embeddings,
        part_bf,
        rel_bf,
        source.reshape(split),
        rel_ids.reshape(split),
        dest.reshape(split),
        negatives.reshape(groups, 1, negs_per),
    )


def flip(me, bit):
    return me + bit * (1 - 2 * ((me // bit) % 2))


def bit_order(me, bits):
    order = [2**t for t in range(bits)]
    if bits > 2:
        core = me % 2
        order[1], order[2] = 2 + 2 * core, 4 - 2 * core
    return order


def slot_of(device, bits):
    slot = device * 0
    for bit in bit_order(device, bits):
        slot = 2 * slot + (device // bit) % 2
    return slot


def greet(me, bits):
    barrier = pltpu.get_barrier_semaphore()
    for t in range(bits):
        pl.semaphore_signal(
            barrier, inc=1, device_id=(flip(me, 2**t),), device_id_type=pl.DeviceIdType.MESH
        )
    pl.semaphore_wait(barrier, bits)


def gather_kernel(bits, shard_ref, out_ref, send_sem, recv_sem):
    me = lax.axis_index("dom")
    slot = slot_of(me, bits)
    order = bit_order(me, bits)
    out_ref[slot] = shard_ref[...]
    greet(me, bits)
    for step in range(bits):
        held = 2**step
        blocks = out_ref.at[pl.ds((slot // held) * held, held)]
        copy = pltpu.make_async_remote_copy(
            src_ref=blocks,
            dst_ref=blocks,
            send_sem=send_sem.at[step],
            recv_sem=recv_sem.at[step],
            device_id=(flip(me, order[bits - 1 - step]),),
            device_id_type=pl.DeviceIdType.MESH,
        )
        copy.start()
        copy.wait()


def gather_relations(shard, size):
    bits = size.bit_length() - 1
    vmem = pl.BlockSpec(memory_space=pltpu.VMEM)
    return pl.pallas_call(
        functools.partial(gather_kernel, bits),
        out_shape=jax.ShapeDtypeStruct((size,) + shard.shape, shard.dtype),
        in_specs=[vmem],
        out_specs=vmem,
        scratch_shapes=[pltpu.SemaphoreType.DMA((bits,)), pltpu.SemaphoreType.DMA((bits,))],
        compiler_params=pltpu.CompilerParams(
            collective_id=0, has_side_effects=True, vmem_limit_bytes=32 * 2**20
        ),
        cost_estimate=pl.CostEstimate(
            flops=0, bytes_accessed=64 * size * shard.size, transcendentals=0
        ),
        name="gather_relations",
    )(shard)


def sum_kernel(bits, grad_ref, out_ref, acc, outgoing, incoming, send_sem, recv_sem):
    me = lax.axis_index("dom")
    order = bit_order(me, bits)
    greet(me, bits)
    source, first = grad_ref, 0
    for step in range(bits):
        half = 2 ** (bits - 1 - step)
        at = 2**bits - 2 * half
        mine = (me // order[step]) % 2
        region = pl.ds(at, half)
        outgoing[region] = source[pl.ds(first + (1 - mine) * half, half)].astype(BF)
        copy = pltpu.make_async_remote_copy(
            src_ref=outgoing.at[region],
            dst_ref=incoming.at[region],
            send_sem=send_sem.at[step],
            recv_sem=recv_sem.at[step],
            device_id=(flip(me, order[step]),),
            device_id_type=pl.DeviceIdType.MESH,
        )
        copy.start()
        copy.wait()
        acc[region] = source[pl.ds(first + mine * half, half)] + incoming[region].astype(F32)
        source, first = acc, at
    out_ref[...] = acc[2**bits - 2]


def sum_relations(grad, size):
    bits = size.bit_length() - 1
    shard = grad.shape[1:]
    vmem = pl.BlockSpec(memory_space=pltpu.VMEM)
    return pl.pallas_call(
        functools.partial(sum_kernel, bits),
        out_shape=jax.ShapeDtypeStruct(shard, F32),
        in_specs=[vmem],
        out_specs=vmem,
        scratch_shapes=[
            pltpu.VMEM(grad.shape, F32),
            pltpu.VMEM(grad.shape, BF),
            pltpu.VMEM(grad.shape, BF),
            pltpu.SemaphoreType.DMA((bits,)),
            pltpu.SemaphoreType.DMA((bits,)),
        ],
        compiler_params=pltpu.CompilerParams(
            collective_id=1, has_side_effects=True, vmem_limit_bytes=50 * 2**20
        ),
        cost_estimate=pl.CostEstimate(
            flops=0, bytes_accessed=64 * grad.size, transcendentals=0
        ),
        name="sum_relations",
    )(grad)


def exchange(value, mask, axis, beside, operand):
    size = lax.axis_size(axis)

    def with_mask(m):
        pairs = [(i, i ^ m) for i in range(size)]
        return lambda v, x: (lax.ppermute(v, axis, pairs), beside(x, size))

    return lax.switch(mask - 1, [with_mask(m) for m in range(1, size)], value, operand)


def adagrad(value, state, grad):
    new_state = state + jnp.mean(grad * grad, axis=1)
    return value - 0.1 * grad / jnp.sqrt(new_state)[:, None], new_state


def local(
    embeddings,
    row_state,
    relations,
    relation_state,
    partner_mask,
    source_rows,
    relation_ids,
    dest_rows,
    negative_rows,
    edge_count,
):
    mask = partner_mask[0]
    size = lax.axis_size("dom")
    share, width = relations.shape
    slots = slot_of(relation_ids // share, size.bit_length() - 1) * share + relation_ids % share
    part_bf, rel_bf = exchange(
        embeddings.astype(BF), mask, "dom", gather_relations, relations.astype(BF)
    )
    rel_bf = rel_bf.reshape(size * share, width)
    own_grad, part_grad, rel_grad = train_bucket(
        embeddings, part_bf, rel_bf, source_rows, slots, dest_rows, negative_rows, edge_count
    )
    returned, rel_share = exchange(
        part_grad, mask, "dom", sum_relations, rel_grad.reshape(size, share, width)
    )
    new_embeddings, new_row_state = adagrad(
        embeddings, row_state, own_grad + returned.astype(F32)
    )
    new_relations, new_relation_state = adagrad(relations, relation_state, rel_share)
    return (new_embeddings, new_row_state, new_relations, new_relation_state)


def solution(mesh):
    in_specs = (
        P("dom", None),
        P("dom"),
        P("dom", None),
        P("dom"),
        P(),
        P("dom"),
        P("dom"),
        P("dom"),
        P("dom", None),
        P("dom"),
    )
    out_specs = (P("dom", None), P("dom"), P("dom", None), P("dom"))
    return jax.shard_map(local, mesh=mesh, in_specs=in_specs, out_specs=out_specs, check_vma=False)
```

```python
import functools

import jax
import jax.numpy as jnp
from jax import lax
from jax.experimental import pallas as pl
from jax.experimental.pallas import tpu as pltpu
from jax.sharding import PartitionSpec as P

BF = jnp.bfloat16
F32 = jnp.float32


def nn(a, b):
    return lax.dot_general(a, b, (((1,), (0,)), ((), ())), preferred_element_type=F32)


def nt(a, b):
    return lax.dot_general(a, b, (((1,), (1,)), ((), ())), preferred_element_type=F32)


def one_hot(rows, ids, first=0):
    at = lax.broadcasted_iota(jnp.int32, (rows, ids.shape[1]), 0) + first
    return at == ids


def as_bf(mask):
    return jnp.where(mask, 1.0, 0.0).astype(BF)


def sigmoid(x):
    return 0.5 * jnp.tanh(0.5 * x) + 0.5


def bucket_kernel(
    count_ref,
    own_ref,
    part_ref,
    rel_ref,
    source_ref,
    ids_ref,
    dest_ref,
    negs_ref,
    own_grad_ref,
    part_grad_ref,
    rel_grad_ref,
    own_t,
    part_t,
    rel_t,
    y_t,
    part_acc,
):
    groups, _, group_len = source_ref.shape
    negs_per = negs_ref.shape[2]
    rows, width = own_ref.shape
    rels = rel_ref.shape[0]
    eye = as_bf(
        lax.broadcasted_iota(jnp.int32, (width, width), 0)
        == lax.broadcasted_iota(jnp.int32, (width, width), 1)
    )
    own_t[...] = nt(eye, own_ref[...].astype(BF)).astype(BF)
    part_t[...] = nt(eye, part_ref[...]).astype(BF)
    rel_t[...] = nt(eye, rel_ref[...]).astype(BF)
    own_grad_ref[...] = jnp.zeros_like(own_grad_ref)
    part_acc[...] = jnp.zeros_like(part_acc)
    count = count_ref[0]

    def group(g, carry):
        from_source = as_bf(one_hot(rows, source_ref[g]))
        own_rows = nn(own_t[...], from_source)
        rel_rows = nn(rel_t[...], as_bf(one_hot(rels, ids_ref[g])))
        queries = (own_rows * rel_rows).astype(BF)
        scores = nn(part_ref[...], queries)
        to_dest = one_hot(rows, dest_ref[g])
        positive = jnp.sum(jnp.where(to_dest, scores, 0.0), axis=0, keepdims=True)
        edge = lax.broadcasted_iota(jnp.int32, (1, group_len), 1) + g * group_len
        live = jnp.where(edge < count, 1.0, 0.0)
        pos_grad = -live * sigmoid(-positive)
        times = jnp.sum(
            jnp.where(one_hot(rows, negs_ref[g]), 1.0 / negs_per, 0.0), axis=1, keepdims=True
        )
        weight = times * (live * sigmoid(scores)) + jnp.where(to_dest, pos_grad, 0.0)
        high = weight.astype(BF)
        low = jnp.where(to_dest, weight - high.astype(F32), 0.0).astype(BF)
        query_grad = nn(part_t[...], high) + nn(part_t[...], low)
        part_acc[...] += nt(high, queries) + nt(low, queries)
        own_grad_ref[...] += nt(from_source, (query_grad * rel_rows).astype(BF))
        columns = pl.ds(pl.multiple_of(g * group_len, group_len), group_len)
        y_t[:, columns] = (query_grad * own_rows).astype(BF)
        return carry

    lax.fori_loop(0, groups, group, 0, unroll=2)
    part_grad_ref[...] = part_acc[...].astype(BF)

    chunk = min(rels, rows)

    def scatter(c, carry):
        first = pl.multiple_of(c * chunk, chunk)
        total = jnp.zeros((chunk, width), F32)
        for g in range(groups):
            hot = as_bf(one_hot(chunk, ids_ref[g], first))
            total = total + nt(hot, y_t[:, g * group_len : (g + 1) * group_len])
        rel_grad_ref[pl.ds(first, chunk), :] = total
        return carry

    lax.fori_loop(0, rels // chunk, scatter, 0)


def train_bucket(embeddings, part_bf, rel_bf, source, rel_ids, dest, negatives, count):
    groups, negs_per = negatives.shape
    edges = source.shape[0]
    rows, width = embeddings.shape
    rels = rel_bf.shape[0]
    split = (groups, 1, edges // groups)
    vmem = pl.BlockSpec(memory_space=pltpu.VMEM)
    unit = 2 * edges * rows * width
    return pl.pallas_call(
        bucket_kernel,
        out_shape=(
            jax.ShapeDtypeStruct((rows, width), F32),
            jax.ShapeDtypeStruct((rows, width), BF),
            jax.ShapeDtypeStruct((rels, width), F32),
        ),
        in_specs=[pl.BlockSpec(memory_space=pltpu.SMEM)] + [vmem] * 7,
        out_specs=(vmem,) * 3,
        scratch_shapes=[
            pltpu.VMEM((width, rows), BF),
            pltpu.VMEM((width, rows), BF),
            pltpu.VMEM((width, rels), BF),
            pltpu.VMEM((width, edges), BF),
            pltpu.VMEM((rows, width), F32),
        ],
        compiler_params=pltpu.CompilerParams(vmem_limit_bytes=50 * 2**20),
        cost_estimate=pl.CostEstimate(
            flops=7 * unit + 2 * unit * rels // rows,
            bytes_accessed=8 * (rows + rels) * width,
            transcendentals=edges * rows,
        ),
        name="bucket",
    )(
        count,
        embeddings,
        part_bf,
        rel_bf,
        source.reshape(split),
        rel_ids.reshape(split),
        dest.reshape(split),
        negatives.reshape(groups, 1, negs_per),
    )


def flip(me, bit):
    return me + bit * (1 - 2 * ((me // bit) % 2))


def bit_order(me, bits):
    order = [2**t for t in range(bits)]
    if bits > 2:
        core = me % 2
        order[1], order[2] = 2 + 2 * core, 4 - 2 * core
    return order


def slot_of(device, bits):
    slot = device * 0
    for bit in bit_order(device, bits):
        slot = 2 * slot + (device // bit) % 2
    return slot


def greet(me, partners):
    barrier = pltpu.get_barrier_semaphore()
    for bit in partners:
        pl.semaphore_signal(
            barrier, inc=1, device_id=(flip(me, bit),), device_id_type=pl.DeviceIdType.MESH
        )
    pl.semaphore_wait(barrier, len(partners))


def gather_kernel(bits, first, last, held_ref, out_ref, send_sem, recv_sem):
    me = lax.axis_index("dom")
    order = bit_order(me, bits)
    slot = slot_of(me, bits) % 2**last
    start = 2**first
    for block in range(start):
        out_ref[(slot // start) * start + block] = held_ref[block]
    greet(me, order[bits - last : bits - first])
    for step in range(first, last):
        held = 2**step
        blocks = out_ref.at[pl.ds((slot // held) * held, held)]
        copy = pltpu.make_async_remote_copy(
            src_ref=blocks,
            dst_ref=blocks,
            send_sem=send_sem.at[step],
            recv_sem=recv_sem.at[step],
            device_id=(flip(me, order[bits - 1 - step]),),
            device_id_type=pl.DeviceIdType.MESH,
        )
        copy.start()
        copy.wait()


def gather_relations(held, size, first, last):
    bits = size.bit_length() - 1
    vmem = pl.BlockSpec(memory_space=pltpu.VMEM)
    return pl.pallas_call(
        functools.partial(gather_kernel, bits, first, last),
        out_shape=jax.ShapeDtypeStruct((2**last,) + held.shape[1:], held.dtype),
        in_specs=[vmem],
        out_specs=vmem,
        scratch_shapes=[pltpu.SemaphoreType.DMA((bits,)), pltpu.SemaphoreType.DMA((bits,))],
        compiler_params=pltpu.CompilerParams(
            collective_id=0 if last == bits else 2,
            has_side_effects=True,
            vmem_limit_bytes=32 * 2**20,
        ),
        cost_estimate=pl.CostEstimate(
            flops=0, bytes_accessed=64 * size * held[0].size, transcendentals=0
        ),
        name="gather_relations",
    )(held)


def sum_kernel(bits, grad_ref, out_ref, acc, outgoing, incoming, send_sem, recv_sem):
    me = lax.axis_index("dom")
    order = bit_order(me, bits)
    greet(me, order)
    source, first = grad_ref, 0
    for step in range(bits):
        half = 2 ** (bits - 1 - step)
        at = 2**bits - 2 * half
        mine = (me // order[step]) % 2
        region = pl.ds(at, half)

        def pack(b, carry, source=source, begin=first + (1 - mine) * half, at=at):
            outgoing[at + b] = source[begin + b].astype(BF)
            return carry

        lax.fori_loop(0, half, pack, 0)
        copy = pltpu.make_async_remote_copy(
            src_ref=outgoing.at[region],
            dst_ref=incoming.at[region],
            send_sem=send_sem.at[step],
            recv_sem=recv_sem.at[step],
            device_id=(flip(me, order[step]),),
            device_id_type=pl.DeviceIdType.MESH,
        )
        copy.start()
        copy.wait()

        def add(b, carry, source=source, begin=first + mine * half, at=at):
            acc[at + b] = source[begin + b] + incoming[at + b].astype(F32)
            return carry

        lax.fori_loop(0, half, add, 0)
        source, first = acc, at
    out_ref[...] = acc[2**bits - 2]


def sum_relations(grad, size):
    bits = size.bit_length() - 1
    shard = grad.shape[1:]
    vmem = pl.BlockSpec(memory_space=pltpu.VMEM)
    return pl.pallas_call(
        functools.partial(sum_kernel, bits),
        out_shape=jax.ShapeDtypeStruct(shard, F32),
        in_specs=[vmem],
        out_specs=vmem,
        scratch_shapes=[
            pltpu.VMEM(grad.shape, F32),
            pltpu.VMEM(grad.shape, BF),
            pltpu.VMEM(grad.shape, BF),
            pltpu.SemaphoreType.DMA((bits,)),
            pltpu.SemaphoreType.DMA((bits,)),
        ],
        compiler_params=pltpu.CompilerParams(
            collective_id=1, has_side_effects=True, vmem_limit_bytes=50 * 2**20
        ),
        cost_estimate=pl.CostEstimate(
            flops=0, bytes_accessed=64 * grad.size, transcendentals=0
        ),
        name="sum_relations",
    )(grad)


def exchange(value, mask, axis, beside, operand):
    size = lax.axis_size(axis)

    def with_mask(m):
        pairs = [(i, i ^ m) for i in range(size)]
        return lambda v, x: (lax.ppermute(v, axis, pairs), beside(x, size))

    return lax.switch(mask - 1, [with_mask(m) for m in range(1, size)], value, operand)


def adagrad(value, state, grad):
    new_state = state + jnp.mean(grad * grad, axis=1)
    return value - 0.1 * grad / jnp.sqrt(new_state)[:, None], new_state


def local(
    embeddings,
    row_state,
    relations,
    relation_state,
    partner_mask,
    source_rows,
    relation_ids,
    dest_rows,
    negative_rows,
    edge_count,
):
    mask = partner_mask[0]
    size = lax.axis_size("dom")
    share, width = relations.shape
    bits = size.bit_length() - 1
    early = max(bits - 3, 0)
    some = relations.astype(BF)[None]
    if early:
        some = gather_relations(some, size, 0, early)

    def gather_rest(held, size):
        return gather_relations(held, size, early, bits)

    part_bf, rel_bf = exchange(
        embeddings.astype(BF), mask, "dom", gather_rest, some
    )
    rel_bf = rel_bf.reshape(size * share, width)
    slots = slot_of(relation_ids // share, bits) * share + relation_ids % share
    own_grad, part_grad, rel_grad = train_bucket(
        embeddings, part_bf, rel_bf, source_rows, slots, dest_rows, negative_rows, edge_count
    )
    returned, rel_share = exchange(
        part_grad, mask, "dom", sum_relations, rel_grad.reshape(size, share, width)
    )
    new_embeddings, new_row_state = adagrad(
        embeddings, row_state, own_grad + returned.astype(F32)
    )
    new_relations, new_relation_state = adagrad(relations, relation_state, rel_share)
    return (new_embeddings, new_row_state, new_relations, new_relation_state)


def solution(mesh):
    in_specs = (
        P("dom", None),
        P("dom"),
        P("dom", None),
        P("dom"),
        P(),
        P("dom"),
        P("dom"),
        P("dom"),
        P("dom", None),
        P("dom"),
    )
    out_specs = (P("dom", None), P("dom"), P("dom", None), P("dom"))
    return jax.shard_map(local, mesh=mesh, in_specs=in_specs, out_specs=out_specs, check_vma=False)
```
